512 devices in a mesh: dp: 8 (over y, core), table: 64 (over x, z).
Axes of the slice: x: 4, y: 4, z: 16, core: 2. Of those that a mesh axis runs over, the one named last changes fastest.
Arguments:
- item_table: bfloat16 [16384, 512], P('table'), may hold values from -6 to 6
- input_weight: bfloat16 [512, 2048], replicated, may hold values from -0.25 to 0.25
- output_weight: bfloat16 [512, 512], replicated, may hold values from -0.25 to 0.25
- request_rows: int32 [512, 64, 4], P(('dp', 'table')), may hold values from 0 to 255
- negative_rows: int32 [512, 64, 1], P(('dp', 'table')), may hold values from 0 to 255
- token_slots: int32 [512, 128], P(('dp', 'table')), may hold values from 0 to 255, as said below
- history_lengths: int32 [512, 4], P(('dp', 'table')), may hold values from 1 to 64, 128 in all within a row
Outputs:
- losses: float32 [65536], P(('dp', 'table'))
- table_grad: float32 [16384, 512], P('table', 'dp')
The draws below stay inside these ranges and needn't reach their ends.
Inputs may be any that keep to these rules, and one draw needn't show every extreme that they name: token_slots points only to live slots: slot s of device d's list to shard o is live when s is below that pair's live count, which is 1 to 4; in every draw one shard receives 4 live slots from every device.
All inputs are finite; a program needn't handle non-finite values.
Results may differ from the reference program's by a relative error of at most 0.014.
Values may be sent and summed in bfloat16 or wider, within the bound.
A program may use at most 64 MiB of HBM per device.

```python
import math
import jax
import jax.numpy as jnp
import numpy as np
from jax import lax

D = 512
HEADS = 4
HEAD = 128
TOK_DEV = 128
SEQS_DEV = 4
MAXLEN = 64
ITEMS_DEV = 256
CAP = 4
NEG_OWN = 1
DEVS = 512
ITEMS = 16384
N_DP = 8
N_TABLE = 64


def owner_counts(key):
    key = jax.random.fold_in(key, 11)
    hot_key, fill_key = jax.random.split(key)
    hottest = jax.random.randint(hot_key, (), 0, N_TABLE)
    counts = jax.random.randint(fill_key, (N_DP * N_TABLE, N_TABLE), 1, CAP + 1)
    return jnp.where(jnp.arange(N_TABLE)[None, :] == hottest, CAP, counts)


def draw_request_rows(key, part):
    key = jax.random.fold_in(key, 3)
    return jax.random.randint(key, (N_DP * N_TABLE, N_TABLE, CAP), 0, ITEMS_DEV).astype(jnp.int32)


def draw_token_slots(key, part):
    counts = owner_counts(key)
    key = jax.random.fold_in(key, 5)
    owner_key, pick_key = jax.random.split(key)
    owners = jax.random.randint(owner_key, (N_DP * N_TABLE, TOK_DEV), 0, N_TABLE)
    picks = jax.random.randint(pick_key, (N_DP * N_TABLE, TOK_DEV), 0, 1 << 20)
    live = jnp.take_along_axis(counts, owners, axis=1)
    ranks = picks % live
    return (owners * CAP + ranks).astype(jnp.int32)


def place_ends(values, rng, smallest, high):
    extent = values.shape
    spot = [jax.random.randint(jax.random.fold_in(rng, axis), (), 0, extent[axis]) for axis in range(len(extent))]
    values = values.at[tuple(spot)].set(smallest)
    longest = extent.index(max(extent))
    spot[longest] = (spot[longest] + 1) % extent[longest]
    return values.at[tuple(spot)].set(high)


def block_scale(stream_key, shape, cuts, least, top_value):
    def one(axis_at, blocks):
        heights = jax.random.uniform(jax.random.fold_in(jax.random.fold_in(stream_key, 6), axis_at), (blocks,), jnp.float32, least / len(cuts), top_value / len(cuts))
        return jnp.repeat(jnp.exp(heights), shape[axis_at] // blocks).reshape((-1,) + (1,) * (len(shape) - axis_at - 1))

    gain = one(*cuts[0])
    for cut in cuts[1:]:
        gain = gain * one(*cut)
    return gain


def split_up(count, total, bound, lean):
    portions = [(1 << 20) // math.isqrt(grade ** lean) + 1 for grade in range(2, count + 1)]
    spare, given = total - bound - (count - 1), [1] * (count - 1)
    while spare > 0:
        candidates = [i for i in range(count - 1) if given[i] < bound]
        pool, budget = sum([portions[i] for i in candidates]), spare
        for i in candidates:
            extra = min(bound - given[i], max(1, budget * portions[i] // pool), spare)
            given[i] = given[i] + extra
            spare = spare - extra
    return np.array([bound] + given)


def uneven(stream_key, count, total, bound, lean):
    if count == 2:
        one = jax.random.randint(stream_key, (), max(1, total - bound), min(bound, total - 1) + 1)
        return jnp.stack([one, total - one])
    sizes = jnp.asarray(split_up(count, total, bound, lean), jnp.int32)
    couples = (count - 1) // 2
    source_of, receiver = sizes[1:1 + 2 * couples:2], sizes[2:2 + 2 * couples:2]
    margin = jnp.minimum(source_of - 1, bound - receiver)
    passed = jax.random.randint(jax.random.fold_in(stream_key, 1), (couples,), 0, 1 << 20) % (margin + 1)
    sizes = sizes.at[1:1 + 2 * couples:2].set(source_of - passed).at[2:2 + 2 * couples:2].set(receiver + passed)
    return sizes[jax.random.permutation(jax.random.fold_in(stream_key, 2), count)]


def scatter_about(key, shape, scale, bound, shards=(), kind=jnp.bfloat16):
    level = block_scale(key, shape, shards, -0.22, 0.18) if shards else 1.0
    result = jax.random.normal(key, shape, jnp.float32) * scale * level
    return jnp.minimum(jnp.maximum(result, -bound), bound).astype(kind)


def setup_inputs(seed: int = 0) -> dict:
    seeds = jax.random.split(jax.random.key(seed), 8)
    item_table = scatter_about(seeds[0], (ITEMS, D), 1.0, 6.0, ((0, 64),))
    input_weight = scatter_about(seeds[1], (D, 4 * D), D ** -0.5, 0.25)
    output_weight = scatter_about(seeds[2], (D, D), D ** -0.5, 0.25)
    request_rows = draw_request_rows(jax.random.fold_in(seeds[7], 71), 0)
    negative_rows = place_ends(jax.random.randint(seeds[4], (DEVS, N_TABLE, NEG_OWN), 0, ITEMS_DEV), jax.random.fold_in(seeds[4], 1), 0, ITEMS_DEV - 1).astype(jnp.int32)
    token_slots = draw_token_slots(jax.random.fold_in(seeds[7], 71), 0)
    history_lengths = jax.vmap(lambda own: uneven(own, SEQS_DEV, TOK_DEV, MAXLEN, 2))(jax.random.split(seeds[6], DEVS)).reshape((DEVS, SEQS_DEV)).astype(jnp.int32)
    return {"item_table": item_table, "input_weight": input_weight, "output_weight": output_weight, "request_rows": request_rows, "negative_rows": negative_rows, "token_slots": token_slots, "history_lengths": history_lengths}


TEMPER = 0.05

def unit_rows(values):
    return values * lax.rsqrt(lax.optimization_barrier(jnp.sum(values * values, axis=-1, keepdims=True)) + 1e-06)

def center(values):
    middle = lax.optimization_barrier(jnp.mean(values, axis=-1, keepdims=True))
    spread = values - middle
    return spread * lax.rsqrt(lax.optimization_barrier(jnp.mean(spread * spread, axis=-1, keepdims=True)) + 1e-05)

def layer_loss(inputs, negatives, lengths_row, input_weight, output_weight):
    rows_here = inputs.shape[0]
    normed = center(inputs).astype(jnp.bfloat16)
    mixed = jax.nn.silu(jnp.dot(normed, input_weight, preferred_element_type=jnp.float32)).astype(jnp.bfloat16)
    gate, values, queries, keys_all = jnp.split(mixed, 4, axis=1)
    ends = jnp.cumsum(lengths_row)
    where_at = jnp.arange(rows_here, dtype=jnp.int32)
    segment = lax.optimization_barrier(jnp.sum((where_at[:, None] >= ends[None, :]).astype(jnp.int32), axis=1))
    allowed = (segment[:, None] == segment[None, :]) & (where_at[None, :] <= where_at[:, None])
    query_h = queries.reshape(rows_here, HEADS, HEAD).astype(jnp.float32)
    key_h = keys_all.reshape(rows_here, HEADS, HEAD).astype(jnp.float32)
    value_h = values.reshape(rows_here, HEADS, HEAD).astype(jnp.float32)
    scores = jnp.einsum('qhd,khd->hqk', query_h, key_h)
    weights = jnp.where(allowed[None], jax.nn.silu(scores * HEAD ** (-0.5)), 0.0) / MAXLEN
    weights = weights.astype(jnp.bfloat16).astype(jnp.float32)
    attended = jnp.einsum('hqk,khd->qhd', weights, value_h).reshape(rows_here, HEADS * HEAD)
    gated = (center(attended) * gate.astype(jnp.float32)).astype(jnp.bfloat16)
    outputs = jnp.dot(gated, output_weight, preferred_element_type=jnp.float32) + inputs
    unit_out = unit_rows(outputs).astype(jnp.bfloat16)
    unit_items = unit_rows(inputs).astype(jnp.bfloat16)
    unit_negs = unit_rows(negatives).astype(jnp.bfloat16)
    target = jnp.concatenate([unit_items[1:], jnp.zeros_like(unit_items[:1])], axis=0)
    positive = lax.optimization_barrier(jnp.sum(unit_out.astype(jnp.float32) * target.astype(jnp.float32), axis=1)) / TEMPER
    negative = lax.dot_general(unit_out, unit_negs, (((1,), (1,)), ((), ())), preferred_element_type=jnp.float32) / TEMPER
    total = jnp.exp(positive) + lax.optimization_barrier(jnp.sum(jnp.exp(negative), axis=1))
    valid = jnp.concatenate([segment[1:] == segment[:-1], jnp.zeros((1,), dtype=bool)])
    return jnp.where(valid, jnp.log(total) - positive, 0.0)

def reference(item_table, input_weight, output_weight, request_rows, negative_rows, token_slots, history_lengths):
    devices_all = N_DP * N_TABLE
    base = (jnp.arange(N_TABLE, dtype=jnp.int32) * ITEMS_DEV)[None, :, None]
    slot_rows = (request_rows + base).reshape(devices_all, N_TABLE * CAP)
    token_rows = jnp.take_along_axis(slot_rows, token_slots.astype(jnp.int32), axis=1)
    neg_global = (negative_rows + base).reshape(N_DP, N_TABLE, N_TABLE * NEG_OWN)
    scored_rows = jnp.transpose(neg_global, (1, 0, 2)).reshape(N_TABLE, N_DP * N_TABLE * NEG_OWN)

    def one_device(grad_total, device):
        item_rows = token_rows[device]
        neg_index = scored_rows[device % N_TABLE]
        inputs = item_table[item_rows].astype(jnp.float32)
        negatives = item_table[neg_index].astype(jnp.float32)

        def local(first, second):
            return layer_loss(first, second, history_lengths[device], input_weight, output_weight)
        device_losses, pullback = jax.vjp(local, inputs, negatives)
        grad_inputs, grad_negs = pullback(jnp.ones_like(device_losses))
        grad_total = grad_total.at[item_rows].add(grad_inputs).at[neg_index].add(grad_negs)
        return (grad_total, device_losses)
    start = jnp.zeros((ITEMS_DEV * N_TABLE, D), jnp.float32)
    grad_total, all_losses = lax.scan(one_device, start, jnp.arange(devices_all, dtype=jnp.int32))
    return (all_losses.reshape(-1), grad_total)
```

```python
import jax
import jax.numpy as jnp
from jax import lax
from jax.experimental import pallas as pl
from jax.experimental.pallas import tpu as pltpu
from jax.sharding import PartitionSpec as P

MESH = pl.DeviceIdType.MESH
BF16 = jnp.bfloat16
F32 = jnp.float32

N_DP = 8
N_TABLE = 64
Z_RING = 16
X_RING = 4
D = 512
HEADS = 4
HEAD = 128
TOK = 128
MAXLEN = 64
CAP = 4
OWN_ITEMS = 256
NEGS = N_DP * N_TABLE
LANES = 128
CHUNKS = D // LANES
TEMPER = 0.05


def dot(a, b, contract=((1,), (0,))):
    return lax.dot_general(a, b, (contract, ((), ())), preferred_element_type=F32)


def rows_to_slabs(value, slab, slots):
    for s in range(slots):
        for c in range(CHUNKS):
            slab[pl.ds(s * CHUNKS + c, N_TABLE, stride=slots * CHUNKS), :] = value[
                s * N_TABLE : (s + 1) * N_TABLE, c * LANES : (c + 1) * LANES
            ]


def slabs_to_rows(slab, slots):
    rows = []
    for s in range(slots):
        parts = [
            slab[pl.ds(s * CHUNKS + c, N_TABLE, stride=slots * CHUNKS), :]
            for c in range(CHUNKS)
        ]
        rows.append(jnp.concatenate(parts, axis=1))
    return rows[0] if slots == 1 else jnp.concatenate(rows, axis=0)


def center_parts(values):
    middle = jnp.mean(values, axis=-1, keepdims=True)
    spread = values - middle
    scale = lax.rsqrt(jnp.mean(spread * spread, axis=-1, keepdims=True) + 1e-05)
    return spread * scale, scale


def center_back(grad, normed, scale):
    first = jnp.mean(grad, axis=-1, keepdims=True)
    second = jnp.mean(grad * normed, axis=-1, keepdims=True)
    return scale * (grad - first - normed * second)


def unit_scale(values):
    return lax.rsqrt(jnp.sum(values * values, axis=-1, keepdims=True) + 1e-06)


def unit_back(grad, values, scale):
    along = jnp.sum(grad * values, axis=-1, keepdims=True)
    return scale * grad - values * (scale * scale * scale * along)


def kernel(
    table_hbm,
    in_weight_hbm,
    out_weight_hbm,
    request_ref,
    negative_ref,
    token_ref,
    length_ref,
    loss_ref,
    grad_ref,
    table_v,
    in_weight,
    out_weight,
    ask_src,
    ask_dst,
    picks,
    picks_t,
    slab_rows,
    slab_negs,
    row_src,
    row_dst,
    neg_src,
    neg_dst,
    unit_all,
    neg_raw,
    neg_out,
    neg_in,
    back_src,
    back_dst,
    neg_back_src,
    neg_back_dst,
    shard_src,
    shard_dst,
    local_sem,
    send_sem,
    recv_sem,
):
    i = lax.axis_index("dp")
    t = lax.axis_index("table")
    tx, tz = t // Z_RING, lax.rem(t, Z_RING)

    def table_peer(k):
        return lax.rem(tx + lax.rem(k, X_RING), X_RING) * Z_RING + lax.rem(
            tz + k // X_RING, Z_RING
        )

    loads = [
        pltpu.make_async_copy(src, dst, local_sem.at[n])
        for n, (src, dst) in enumerate(
            ((table_hbm, table_v), (in_weight_hbm, in_weight), (out_weight_hbm, out_weight))
        )
    ]
    for load in loads:
        load.start()

    barrier = pltpu.get_barrier_semaphore()

    def greet(k, carry):
        pl.semaphore_signal(
            barrier, inc=1, device_id={"table": table_peer(k)}, device_id_type=MESH
        )
        return carry

    lax.fori_loop(1, N_TABLE, greet, 0)
    for k in range(1, N_DP):
        pl.semaphore_signal(
            barrier, inc=1, device_id={"dp": lax.rem(i + k, N_DP)}, device_id_type=MESH
        )

    def send_table(src, dst, n):
        def step(k, carry):
            peer = table_peer(k)
            pltpu.make_async_remote_copy(
                src_ref=src.at[peer],
                dst_ref=dst.at[t],
                send_sem=send_sem.at[n],
                recv_sem=recv_sem.at[n],
                device_id={"table": peer},
                device_id_type=MESH,
            ).start()
            return carry

        lax.fori_loop(1, N_TABLE, step, 0)

    def send_dp(src_of, dst, n):
        for k in range(1, N_DP):
            peer = lax.rem(i + k, N_DP)
            pltpu.make_async_remote_copy(
                src_ref=src_of(peer),
                dst_ref=dst,
                send_sem=send_sem.at[n],
                recv_sem=recv_sem.at[n],
                device_id={"dp": peer},
                device_id_type=MESH,
            ).start()

    def wait_all(ref, count, n):
        part = ref.at[pl.ds(0, count)]
        pltpu.make_async_copy(part, part, recv_sem.at[n]).wait()

    def wait_sent(ref, count, n):
        part = ref.at[pl.ds(0, count)]
        pltpu.make_async_copy(part, part, send_sem.at[n]).wait()

    lane = lax.broadcasted_iota(jnp.int32, (N_TABLE, LANES), 1)
    asks = jnp.zeros((N_TABLE, LANES), jnp.int32)
    for s in range(CAP):
        asks = jnp.where(lane == s, request_ref[0, :, s : s + 1], asks)
    asks = jnp.where(lane == CAP, negative_ref[0, :, 0:1], asks)
    ask_src[:, 0, :] = asks
    ask_dst[pl.ds(t, 1)] = ask_src[pl.ds(t, 1)]
    pl.semaphore_wait(barrier, N_TABLE - 1 + N_DP - 1)
    send_table(ask_src, ask_dst, 0)

    sub_tok = lax.broadcasted_iota(jnp.int32, (TOK, TOK), 0)
    lane_tok = lax.broadcasted_iota(jnp.int32, (TOK, TOK), 1)
    seg_q = jnp.zeros((TOK, TOK), jnp.int32)
    seg_k = jnp.zeros((TOK, TOK), jnp.int32)
    seg_next = jnp.zeros((TOK, TOK), jnp.int32)
    end = jnp.int32(0)
    for n in range(length_ref.shape[1]):
        end = end + length_ref[0, n]
        seg_q = seg_q + (sub_tok >= end).astype(jnp.int32)
        seg_k = seg_k + (lane_tok >= end).astype(jnp.int32)
        seg_next = seg_next + (sub_tok + 1 >= end).astype(jnp.int32)
    allowed = (seg_q == seg_k) & (lane_tok <= sub_tok)
    valid = ((seg_q == seg_next) & (sub_tok < TOK - 1))[:, 0:1]
    slots = token_ref[...]
    place = (slots & (CAP - 1)) * N_TABLE + slots // CAP
    token_t = (
        lax.broadcasted_iota(jnp.int32, (CAP * N_TABLE, TOK), 0) == place
    ).astype(F32)
    token_pick = jnp.transpose(token_t).astype(BF16)
    token_t = token_t.astype(BF16)

    loads[0].wait()
    wait_all(ask_dst, N_TABLE - 1, 0)
    asked = ask_dst[:, 0, :]
    item = lax.broadcasted_iota(jnp.int32, (N_TABLE, OWN_ITEMS), 1)
    for s in range(CAP + 1):
        picks[s * N_TABLE : (s + 1) * N_TABLE, :] = (
            (asked[:, s : s + 1] == item).astype(F32).astype(BF16)
        )
    own_table = table_v[...]
    found_negs = dot(picks[CAP * N_TABLE :, :], own_table)
    for c in range(CHUNKS):
        slab_negs[:, c, :] = found_negs[:, c * LANES : (c + 1) * LANES]
    neg_src[...] = slab_negs[...].astype(BF16)
    neg_dst[pl.ds(t, 1)] = neg_src[pl.ds(t, 1)]
    send_table(neg_src, neg_dst, 1)
    rows_to_slabs(dot(picks[: CAP * N_TABLE, :], own_table), slab_rows, CAP)
    row_src[...] = slab_rows[...].astype(BF16).reshape(row_src.shape)
    row_dst[pl.ds(t, 1)] = row_src[pl.ds(t, 1)]
    send_table(row_src, row_dst, 2)
    picks_t[...] = jnp.transpose(picks[...].astype(F32)).astype(BF16)

    wait_all(neg_dst, N_TABLE - 1, 1)
    slab_negs[...] = neg_dst[...].astype(F32)
    negs = jnp.concatenate([slab_negs[:, c, :] for c in range(CHUNKS)], axis=1)
    neg_raw[...] = negs
    unit_all[pl.ds(i, 1)] = (negs * unit_scale(negs)).astype(BF16)[None]
    send_dp(lambda peer: unit_all.at[i], unit_all.at[i], 3)
    loads[1].wait()
    loads[2].wait()

    wait_all(row_dst, N_TABLE - 1, 2)
    slab_rows[...] = row_dst[...].reshape(slab_rows.shape).astype(F32)
    history = slabs_to_rows(slab_rows, CAP).astype(BF16)
    inputs = dot(token_pick, history)
    normed, in_scale = center_parts(inputs)
    pre = dot(normed.astype(BF16), in_weight[...])
    sig = jax.nn.sigmoid(pre)
    mixed = (pre * sig).astype(BF16)
    gate, values, queries, keys = (mixed[:, n * D : (n + 1) * D] for n in range(4))
    raw, weights, attended = [], [], []
    for h in range(HEADS):
        at = slice(h * HEAD, (h + 1) * HEAD)
        scores = dot(queries[:, at], keys[:, at], ((1,), (1,))) * HEAD ** (-0.5)
        raw.append(scores)
        weight = jnp.where(allowed, scores * jax.nn.sigmoid(scores), 0.0) / MAXLEN
        weights.append(weight.astype(BF16))
        attended.append(dot(weights[h], values[:, at]))
    att_normed, att_scale = center_parts(jnp.concatenate(attended, axis=1))
    gate32 = gate.astype(F32)
    gated = (att_normed * gate32).astype(BF16)
    outputs = dot(gated, out_weight[...]) + inputs
    out_scale = unit_scale(outputs)
    unit_out = (outputs * out_scale).astype(BF16)
    item_scale = unit_scale(inputs)
    unit_items = (inputs * item_scale).astype(BF16).astype(F32)
    target = pltpu.roll(unit_items, TOK - 1, 0)
    unit_out32 = unit_out.astype(F32)
    positive = jnp.sum(unit_out32 * target, axis=1, keepdims=True) / TEMPER

    wait_all(unit_all, N_DP - 1, 3)
    unit_negs = unit_all[...].reshape(NEGS, D)
    exp_neg = jnp.exp(dot(unit_out, unit_negs, ((1,), (1,))) / TEMPER)
    exp_pos = jnp.exp(positive)
    total = exp_pos + jnp.sum(exp_neg, axis=1, keepdims=True)
    loss = jnp.where(valid, jnp.log(total) - positive, 0.0)
    loss_ref[...] = jnp.transpose(jnp.broadcast_to(loss, (TOK, LANES)))[0:1, :]

    per_row = jnp.where(valid, 1.0 / (total * TEMPER), 0.0)
    d_neg = (exp_neg * per_row).astype(BF16)
    d_pos = jnp.where(valid, exp_pos * per_row - 1.0 / TEMPER, 0.0)
    neg_out[...] = dot(d_neg, unit_out, ((0,), (0,))).astype(BF16).reshape(neg_out.shape)
    send_dp(lambda peer: neg_out.at[peer], neg_in.at[i], 4)
    neg_in[pl.ds(i, 1)] = neg_out[pl.ds(i, 1)]

    d_unit_out = dot(d_neg, unit_negs) + d_pos * target
    d_outputs = unit_back(d_unit_out, outputs, out_scale)
    d_unit_items = pltpu.roll(d_pos * unit_out32, 1, 0)
    d_inputs = d_outputs + unit_back(d_unit_items, inputs, item_scale)

    d_gated = dot(d_outputs.astype(BF16), out_weight[...], ((1,), (1,)))
    d_gate = d_gated * att_normed
    d_att = center_back(d_gated * gate32, att_normed, att_scale).astype(BF16)
    d_values, d_queries, d_keys = [], [], []
    for h in range(HEADS):
        at = slice(h * HEAD, (h + 1) * HEAD)
        d_weight = dot(d_att[:, at], values[:, at], ((1,), (1,)))
        d_values.append(dot(weights[h], d_att[:, at], ((0,), (0,))))
        s_sig = jax.nn.sigmoid(raw[h])
        slope = s_sig * (1.0 + raw[h] * (1.0 - s_sig))
        d_scores = jnp.where(
            allowed, d_weight * slope * (HEAD ** (-0.5) / MAXLEN), 0.0
        ).astype(BF16)
        d_queries.append(dot(d_scores, keys[:, at]))
        d_keys.append(dot(d_scores, queries[:, at], ((0,), (0,))))
    d_mixed = jnp.concatenate([d_gate] + d_values + d_queries + d_keys, axis=1)
    d_pre = (d_mixed * (sig * (1.0 + pre * (1.0 - sig)))).astype(BF16)
    d_normed = dot(d_pre, in_weight[...], ((1,), (1,)))
    d_inputs = d_inputs + center_back(d_normed, normed, in_scale)

    wait_all(neg_in, N_DP - 1, 4)
    d_units = jnp.sum(neg_in[...].astype(F32), axis=0)
    own_negs = neg_raw[...]
    d_negs = unit_back(d_units, own_negs, unit_scale(own_negs))
    for c in range(CHUNKS):
        slab_negs[:, c, :] = d_negs[:, c * LANES : (c + 1) * LANES]
    neg_back_src[...] = slab_negs[...].astype(BF16)
    neg_back_dst[pl.ds(t, 1)] = neg_back_src[pl.ds(t, 1)]
    send_table(neg_back_src, neg_back_dst, 5)

    rows_to_slabs(dot(token_t, d_inputs.astype(BF16)), slab_rows, CAP)
    back_src[...] = slab_rows[...].astype(BF16).reshape(back_src.shape)
    back_dst[pl.ds(t, 1)] = back_src[pl.ds(t, 1)]
    send_table(back_src, back_dst, 6)

    wait_all(neg_back_dst, N_TABLE - 1, 5)
    slab_negs[...] = neg_back_dst[...].astype(F32)
    back_negs = jnp.concatenate([slab_negs[:, c, :] for c in range(CHUNKS)], axis=1)
    shard_negs = dot(picks_t[:, CAP * N_TABLE :], back_negs.astype(BF16))
    wait_all(back_dst, N_TABLE - 1, 6)
    slab_rows[...] = back_dst[...].reshape(slab_rows.shape).astype(F32)
    back_rows = slabs_to_rows(slab_rows, CAP).astype(BF16)
    shard = shard_negs + dot(picks_t[:, : CAP * N_TABLE], back_rows)

    half = OWN_ITEMS // 2
    left = lax.broadcasted_iota(jnp.int32, (half, LANES), 1) < LANES // 2
    for c in range(CHUNKS):
        top = shard[:half, c * LANES : (c + 1) * LANES]
        low = shard[half:, c * LANES : (c + 1) * LANES]
        top_r, low_r = pltpu.roll(top, LANES // 2, 1), pltpu.roll(low, LANES // 2, 1)
        shard_src[2 * c] = jnp.where(left, top, low_r).astype(BF16)
        shard_src[2 * c + 1] = jnp.where(left, top_r, low).astype(BF16)
    send_dp(lambda peer: shard_src.at[peer], shard_dst.at[i], 7)
    shard_dst[pl.ds(i, 1)] = shard_src[pl.ds(i, 1)]

    wait_sent(ask_src, N_TABLE - 1, 0)
    wait_sent(neg_src, N_TABLE - 1, 1)
    wait_sent(row_src, N_TABLE - 1, 2)
    wait_sent(unit_all, N_DP - 1, 3)
    wait_sent(neg_out, N_DP - 1, 4)
    wait_sent(neg_back_src, N_TABLE - 1, 5)
    wait_sent(back_src, N_TABLE - 1, 6)
    wait_sent(shard_src, N_DP - 1, 7)
    wait_all(shard_dst, N_DP - 1, 7)
    summed = jnp.sum(shard_dst[...].astype(F32), axis=0)
    grad_ref[:half, :] = summed[:, : LANES // 2]
    grad_ref[half:, :] = pltpu.roll(summed, LANES // 2, 1)[:, : LANES // 2]


def body(
    item_table,
    input_weight,
    output_weight,
    request_rows,
    negative_rows,
    token_slots,
    history_lengths,
):
    vmem = pl.BlockSpec(memory_space=pltpu.VMEM)
    smem = pl.BlockSpec(memory_space=pltpu.SMEM)
    anywhere = pl.BlockSpec(memory_space=pl.ANY)
    loss, grad = pl.pallas_call(
        kernel,
        name="hstu_step",
        out_shape=(
            jax.ShapeDtypeStruct((1, TOK), F32),
            jax.ShapeDtypeStruct((OWN_ITEMS, D // N_DP), F32),
        ),
        in_specs=[anywhere, anywhere, anywhere, vmem, vmem, vmem, smem],
        out_specs=(vmem, vmem),
        scratch_shapes=[
            pltpu.VMEM((OWN_ITEMS, D), BF16),
            pltpu.VMEM((D, 4 * D), BF16),
            pltpu.VMEM((D, D), BF16),
            pltpu.VMEM((N_TABLE, 1, LANES), jnp.int32),
            pltpu.VMEM((N_TABLE, 1, LANES), jnp.int32),
            pltpu.VMEM(((CAP + 1) * N_TABLE, OWN_ITEMS), BF16),
            pltpu.VMEM((OWN_ITEMS, (CAP + 1) * N_TABLE), BF16),
            pltpu.VMEM((N_TABLE * CAP * CHUNKS, LANES), F32),
            pltpu.VMEM((N_TABLE, CHUNKS, LANES), F32),
            pltpu.VMEM((N_TABLE, CAP * CHUNKS, LANES), BF16),
            pltpu.VMEM((N_TABLE, CAP * CHUNKS, LANES), BF16),
            pltpu.VMEM((N_TABLE, CHUNKS, LANES), BF16),
            pltpu.VMEM((N_TABLE, CHUNKS, LANES), BF16),
            pltpu.VMEM((N_DP, N_TABLE, D), BF16),
            pltpu.VMEM((N_TABLE, D), F32),
            pltpu.VMEM((N_DP, N_TABLE, D), BF16),
            pltpu.VMEM((N_DP, N_TABLE, D), BF16),
            pltpu.VMEM((N_TABLE, CAP * CHUNKS, LANES), BF16),
            pltpu.VMEM((N_TABLE, CAP * CHUNKS, LANES), BF16),
            pltpu.VMEM((N_TABLE, CHUNKS, LANES), BF16),
            pltpu.VMEM((N_TABLE, CHUNKS, LANES), BF16),
            pltpu.VMEM((N_DP, OWN_ITEMS // 2, LANES), BF16),
            pltpu.VMEM((N_DP, OWN_ITEMS // 2, LANES), BF16),
            pltpu.SemaphoreType.DMA((3,)),
            pltpu.SemaphoreType.DMA((8,)),
            pltpu.SemaphoreType.DMA((8,)),
        ],
        compiler_params=pltpu.CompilerParams(
            collective_id=0, has_side_effects=True, vmem_limit_bytes=48 * 2**20
        ),
    )(
        item_table,
        input_weight,
        output_weight,
        request_rows,
        negative_rows,
        token_slots,
        history_lengths,
    )
    return loss.reshape(TOK), grad


def solution(mesh):
    placed = (
        P("table", None),
        P(),
        P(),
        P(("dp", "table"), None, None),
        P(("dp", "table"), None, None),
        P(("dp", "table"), None),
        P(("dp", "table"), None),
    )
    return jax.shard_map(
        body,
        mesh=mesh,
        in_specs=placed,
        out_specs=(P(("dp", "table")), P("table", "dp")),
        check_vma=False,
    )
```

```python
import jax
import jax.numpy as jnp
from jax import lax
from jax.experimental import pallas as pl
from jax.experimental.pallas import tpu as pltpu
from jax.sharding import PartitionSpec as P

MESH = pl.DeviceIdType.MESH
BF16 = jnp.bfloat16
F32 = jnp.float32

N_DP = 8
N_TABLE = 64
Z_RING = 16
X_RING = 4
D = 512
HEADS = 4
HEAD = 128
TOK = 128
MAXLEN = 64
SEQS = 4
CAP = 4
OWN_ITEMS = 256
NEGS = N_DP * N_TABLE
LANES = 128
CHUNKS = D // LANES
TEMPER = 0.05


OFFSETS = sorted(
    ((x, z) for x in range(X_RING) for z in range(Z_RING) if x or z),
    key=lambda o: -(min(o[0], X_RING - o[0]) + min(o[1], Z_RING - o[1])),
)


def dot(a, b, contract=((1,), (0,))):
    return lax.dot_general(a, b, (contract, ((), ())), preferred_element_type=F32)


def rows_to_slabs(value, slab, slots):
    for s in range(slots):
        for c in range(CHUNKS):
            slab[pl.ds(s * CHUNKS + c, N_TABLE, stride=slots * CHUNKS), :] = value[
                s * N_TABLE : (s + 1) * N_TABLE, c * LANES : (c + 1) * LANES
            ]


def slabs_to_rows(slab, slots):
    rows = []
    for s in range(slots):
        parts = [
            slab[pl.ds(s * CHUNKS + c, N_TABLE, stride=slots * CHUNKS), :]
            for c in range(CHUNKS)
        ]
        rows.append(jnp.concatenate(parts, axis=1))
    return rows[0] if slots == 1 else jnp.concatenate(rows, axis=0)


def center_parts(values):
    middle = jnp.mean(values, axis=-1, keepdims=True)
    spread = values - middle
    scale = lax.rsqrt(jnp.mean(spread * spread, axis=-1, keepdims=True) + 1e-05)
    return spread * scale, scale


def center_back(grad, normed, scale):
    first = jnp.mean(grad, axis=-1, keepdims=True)
    second = jnp.mean(grad * normed, axis=-1, keepdims=True)
    return scale * (grad - first - normed * second)


def unit_scale(values):
    return lax.rsqrt(jnp.sum(values * values, axis=-1, keepdims=True) + 1e-06)


def unit_back(grad, values, scale):
    along = jnp.sum(grad * values, axis=-1, keepdims=True)
    return scale * grad - values * (scale * scale * scale * along)


def kernel(
    request_hbm,
    negative_hbm,
    token_hbm,
    table_hbm,
    in_weight_hbm,
    out_weight_hbm,
    length_hbm,
    loss_ref,
    grad_ref,
    request_v,
    token_v,
    length_ref,
    table_v,
    in_weight,
    out_weight,
    ask_src,
    ask_dst,
    picks,
    picks_t,
    slab_rows,
    slab_negs,
    row_src,
    row_dst,
    neg_src,
    neg_dst,
    unit_all,
    neg_raw,
    neg_out,
    neg_in,
    back_src,
    back_dst,
    neg_back_src,
    neg_back_dst,
    shard_src,
    shard_dst,
    local_sem,
    send_sem,
    recv_sem,
):
    i = lax.axis_index("dp")
    t = lax.axis_index("table")
    tx, tz = t // Z_RING, lax.rem(t, Z_RING)

    def table_peer(offset):
        return lax.rem(tx + offset[0], X_RING) * Z_RING + lax.rem(tz + offset[1], Z_RING)

    loads = [
        pltpu.make_async_copy(src, dst, local_sem.at[n])
        for n, (src, dst) in enumerate(
            (
                (request_hbm, request_v.at[pl.ds(0, CAP)]),
                (negative_hbm, request_v.at[pl.ds(CAP, 1)]),
                (token_hbm, token_v),
                (table_hbm, table_v),
                (in_weight_hbm, in_weight),
                (out_weight_hbm, out_weight),
                (length_hbm, length_ref),
            )
        )
    ]
    for load in loads:
        load.start()

    barrier = pltpu.get_barrier_semaphore()

    for offset in OFFSETS:
        pl.semaphore_signal(
            barrier, inc=1, device_id={"table": table_peer(offset)}, device_id_type=MESH
        )
    for k in range(1, N_DP):
        pl.semaphore_signal(
            barrier, inc=1, device_id={"dp": lax.rem(i + k, N_DP)}, device_id_type=MESH
        )

    def send_table(src, dst, n):
        for offset in OFFSETS:
            peer = table_peer(offset)
            pltpu.make_async_remote_copy(
                src_ref=src.at[peer],
                dst_ref=dst.at[t],
                send_sem=send_sem.at[n],
                recv_sem=recv_sem.at[n],
                device_id={"table": peer},
                device_id_type=MESH,
            ).start()

    def send_dp(src_of, dst, n):
        for k in range(1, N_DP):
            peer = lax.rem(i + k, N_DP)
            pltpu.make_async_remote_copy(
                src_ref=src_of(peer),
                dst_ref=dst,
                send_sem=send_sem.at[n],
                recv_sem=recv_sem.at[n],
                device_id={"dp": peer},
                device_id_type=MESH,
            ).start()

    def wait_all(ref, count, n):
        part = ref.at[pl.ds(0, count)]
        pltpu.make_async_copy(part, part, recv_sem.at[n]).wait()

    def wait_sent(ref, count, n):
        part = ref.at[pl.ds(0, count)]
        pltpu.make_async_copy(part, part, send_sem.at[n]).wait()

    loads[0].wait()
    loads[1].wait()
    asks = jnp.concatenate(
        [request_v[0 : CAP + 1, :], jnp.zeros((LANES - CAP - 1, N_TABLE), jnp.int32)], axis=0
    )
    ask_src[:, 0, :] = jnp.transpose(asks.astype(F32)).astype(jnp.int32)
    ask_dst[pl.ds(t, 1)] = ask_src[pl.ds(t, 1)]
    pl.semaphore_wait(barrier, N_TABLE - 1 + N_DP - 1)
    send_table(ask_src, ask_dst, 0)

    sub_tok = lax.broadcasted_iota(jnp.int32, (TOK, TOK), 0)
    lane_tok = lax.broadcasted_iota(jnp.int32, (TOK, TOK), 1)
    loads[6].wait()
    seg_q = jnp.zeros((TOK, TOK), jnp.int32)
    seg_k = jnp.zeros((TOK, TOK), jnp.int32)
    seg_next = jnp.zeros((TOK, TOK), jnp.int32)
    end = jnp.int32(0)
    for n in range(length_ref.shape[1]):
        end = end + length_ref[0, n]
        seg_q = seg_q + (sub_tok >= end).astype(jnp.int32)
        seg_k = seg_k + (lane_tok >= end).astype(jnp.int32)
        seg_next = seg_next + (sub_tok + 1 >= end).astype(jnp.int32)
    allowed = (seg_q == seg_k) & (lane_tok <= sub_tok)
    valid = ((seg_q == seg_next) & (sub_tok < TOK - 1))[:, 0:1]
    loads[2].wait()
    slots = token_v[...]
    place = (slots & (CAP - 1)) * N_TABLE + slots // CAP
    token_t = (
        lax.broadcasted_iota(jnp.int32, (CAP * N_TABLE, TOK), 0) == place
    ).astype(F32)
    token_pick = jnp.transpose(token_t).astype(BF16)
    token_t = token_t.astype(BF16)

    loads[3].wait()
    wait_all(ask_dst, N_TABLE - 1, 0)
    asked = ask_dst[:, 0, :]
    item = lax.broadcasted_iota(jnp.int32, (N_TABLE, OWN_ITEMS), 1)
    for s in range(CAP + 1):
        picks[s * N_TABLE : (s + 1) * N_TABLE, :] = (
            (asked[:, s : s + 1] == item).astype(F32).astype(BF16)
        )
    own_table = table_v[...]
    found_negs = dot(picks[CAP * N_TABLE :, :], own_table)
    for c in range(CHUNKS):
        slab_negs[:, c, :] = found_negs[:, c * LANES : (c + 1) * LANES]
    neg_src[...] = slab_negs[...].astype(BF16)
    neg_dst[pl.ds(t, 1)] = neg_src[pl.ds(t, 1)]
    send_table(neg_src, neg_dst, 1)
    rows_to_slabs(dot(picks[: CAP * N_TABLE, :], own_table), slab_rows, CAP)
    row_src[...] = slab_rows[...].astype(BF16).reshape(row_src.shape)
    row_dst[pl.ds(t, 1)] = row_src[pl.ds(t, 1)]
    send_table(row_src, row_dst, 2)
    picks_t[...] = jnp.transpose(picks[...].astype(F32)).astype(BF16)

    wait_all(neg_dst, N_TABLE - 1, 1)
    slab_negs[...] = neg_dst[...].astype(F32)
    negs = jnp.concatenate([slab_negs[:, c, :] for c in range(CHUNKS)], axis=1)
    neg_raw[...] = negs
    unit_all[pl.ds(i, 1)] = (negs * unit_scale(negs)).astype(BF16)[None]
    send_dp(lambda peer: unit_all.at[i], unit_all.at[i], 3)
    loads[4].wait()
    loads[5].wait()

    wait_all(row_dst, N_TABLE - 1, 2)
    slab_rows[...] = row_dst[...].reshape(slab_rows.shape).astype(F32)
    history = slabs_to_rows(slab_rows, CAP).astype(BF16)
    inputs = dot(token_pick, history)
    normed, in_scale = center_parts(inputs)
    pre = dot(normed.astype(BF16), in_weight[...])
    sig = jax.nn.sigmoid(pre)
    mixed = (pre * sig).astype(BF16)
    gate, values, queries, keys = (mixed[:, n * D : (n + 1) * D] for n in range(4))
    raw, weights, attended = [], [], []
    for h in range(HEADS):
        at = slice(h * HEAD, (h + 1) * HEAD)
        scores = dot(queries[:, at], keys[:, at], ((1,), (1,))) * HEAD ** (-0.5)
        raw.append(scores)
        weight = jnp.where(allowed, scores * jax.nn.sigmoid(scores), 0.0) / MAXLEN
        weights.append(weight.astype(BF16))
        attended.append(dot(weights[h], values[:, at]))
    att_normed, att_scale = center_parts(jnp.concatenate(attended, axis=1))
    gate32 = gate.astype(F32)
    gated = (att_normed * gate32).astype(BF16)
    outputs = dot(gated, out_weight[...]) + inputs
    out_scale = unit_scale(outputs)
    unit_out = (outputs * out_scale).astype(BF16)
    item_scale = unit_scale(inputs)
    unit_items = (inputs * item_scale).astype(BF16).astype(F32)
    target = pltpu.roll(unit_items, TOK - 1, 0)
    unit_out32 = unit_out.astype(F32)
    positive = jnp.sum(unit_out32 * target, axis=1, keepdims=True) / TEMPER

    wait_all(unit_all, N_DP - 1, 3)
    unit_negs = unit_all[...].reshape(NEGS, D)
    exp_neg = jnp.exp(dot(unit_out, unit_negs, ((1,), (1,))) / TEMPER)
    exp_pos = jnp.exp(positive)
    total = exp_pos + jnp.sum(exp_neg, axis=1, keepdims=True)
    loss = jnp.where(valid, jnp.log(total) - positive, 0.0)
    loss_ref[...] = jnp.transpose(jnp.broadcast_to(loss, (TOK, LANES)))[0:1, :]

    per_row = jnp.where(valid, 1.0 / (total * TEMPER), 0.0)
    d_neg = (exp_neg * per_row).astype(BF16)
    d_pos = jnp.where(valid, exp_pos * per_row - 1.0 / TEMPER, 0.0)
    neg_out[...] = dot(d_neg, unit_out, ((0,), (0,))).astype(BF16).reshape(neg_out.shape)
    send_dp(lambda peer: neg_out.at[peer], neg_in.at[i], 4)
    neg_in[pl.ds(i, 1)] = neg_out[pl.ds(i, 1)]

    d_unit_out = dot(d_neg, unit_negs) + d_pos * target
    d_outputs = unit_back(d_unit_out, outputs, out_scale)
    d_unit_items = pltpu.roll(d_pos * unit_out32, 1, 0)
    d_inputs = d_outputs + unit_back(d_unit_items, inputs, item_scale)

    d_gated = dot(d_outputs.astype(BF16), out_weight[...], ((1,), (1,)))
    d_gate = d_gated * att_normed
    d_att = center_back(d_gated * gate32, att_normed, att_scale).astype(BF16)
    d_values, d_queries, d_keys = [], [], []
    for h in range(HEADS):
        at = slice(h * HEAD, (h + 1) * HEAD)
        d_weight = dot(d_att[:, at], values[:, at], ((1,), (1,)))
        d_values.append(dot(weights[h], d_att[:, at], ((0,), (0,))))
        s_sig = jax.nn.sigmoid(raw[h])
        slope = s_sig * (1.0 + raw[h] * (1.0 - s_sig))
        d_scores = jnp.where(
            allowed, d_weight * slope * (HEAD ** (-0.5) / MAXLEN), 0.0
        ).astype(BF16)
        d_queries.append(dot(d_scores, keys[:, at]))
        d_keys.append(dot(d_scores, queries[:, at], ((0,), (0,))))
    d_mixed = jnp.concatenate([d_gate] + d_values + d_queries + d_keys, axis=1)
    d_pre = (d_mixed * (sig * (1.0 + pre * (1.0 - sig)))).astype(BF16)
    d_normed = dot(d_pre, in_weight[...], ((1,), (1,)))
    d_inputs = d_inputs + center_back(d_normed, normed, in_scale)

    rows_to_slabs(dot(token_t, d_inputs.astype(BF16)), slab_rows, CAP)
    back_src[...] = slab_rows[...].astype(BF16).reshape(back_src.shape)
    back_dst[pl.ds(t, 1)] = back_src[pl.ds(t, 1)]
    send_table(back_src, back_dst, 6)

    wait_all(neg_in, N_DP - 1, 4)
    d_units = jnp.sum(neg_in[...].astype(F32), axis=0)
    own_negs = neg_raw[...]
    d_negs = unit_back(d_units, own_negs, unit_scale(own_negs))
    for c in range(CHUNKS):
        slab_negs[:, c, :] = d_negs[:, c * LANES : (c + 1) * LANES]
    neg_back_src[...] = slab_negs[...].astype(BF16)
    neg_back_dst[pl.ds(t, 1)] = neg_back_src[pl.ds(t, 1)]
    send_table(neg_back_src, neg_back_dst, 5)

    wait_all(neg_back_dst, N_TABLE - 1, 5)
    slab_negs[...] = neg_back_dst[...].astype(F32)
    back_negs = jnp.concatenate([slab_negs[:, c, :] for c in range(CHUNKS)], axis=1)
    shard_negs = dot(picks_t[:, CAP * N_TABLE :], back_negs.astype(BF16))
    wait_all(back_dst, N_TABLE - 1, 6)
    slab_rows[...] = back_dst[...].reshape(slab_rows.shape).astype(F32)
    back_rows = slabs_to_rows(slab_rows, CAP).astype(BF16)
    shard = shard_negs + dot(picks_t[:, : CAP * N_TABLE], back_rows)

    half = OWN_ITEMS // 2
    left = lax.broadcasted_iota(jnp.int32, (half, LANES), 1) < LANES // 2
    for c in range(CHUNKS):
        top = shard[:half, c * LANES : (c + 1) * LANES]
        low = shard[half:, c * LANES : (c + 1) * LANES]
        top_r, low_r = pltpu.roll(top, LANES // 2, 1), pltpu.roll(low, LANES // 2, 1)
        shard_src[2 * c] = jnp.where(left, top, low_r).astype(BF16)
        shard_src[2 * c + 1] = jnp.where(left, top_r, low).astype(BF16)
    send_dp(lambda peer: shard_src.at[peer], shard_dst.at[i], 7)
    shard_dst[pl.ds(i, 1)] = shard_src[pl.ds(i, 1)]

    wait_sent(ask_src, N_TABLE - 1, 0)
    wait_sent(neg_src, N_TABLE - 1, 1)
    wait_sent(row_src, N_TABLE - 1, 2)
    wait_sent(unit_all, N_DP - 1, 3)
    wait_sent(neg_out, N_DP - 1, 4)
    wait_sent(neg_back_src, N_TABLE - 1, 5)
    wait_sent(back_src, N_TABLE - 1, 6)
    wait_sent(shard_src, N_DP - 1, 7)
    wait_all(shard_dst, N_DP - 1, 7)
    summed = jnp.sum(shard_dst[...].astype(F32), axis=0)
    turned = jnp.transpose(summed)
    grad_ref[:, :half] = turned[: LANES // 2, :]
    grad_ref[:, half:] = turned[LANES // 2 :, :]


def body(
    item_table,
    input_weight,
    output_weight,
    request_rows,
    negative_rows,
    token_slots,
    history_lengths,
):
    vmem = pl.BlockSpec(memory_space=pltpu.VMEM)
    anywhere = pl.BlockSpec(memory_space=pl.ANY)
    loss, grad = pl.pallas_call(
        kernel,
        name="hstu_step",
        out_shape=(
            jax.ShapeDtypeStruct((1, TOK), F32),
            jax.ShapeDtypeStruct((D // N_DP, OWN_ITEMS), F32),
        ),
        in_specs=[anywhere] * 7,
        out_specs=(vmem, vmem),
        scratch_shapes=[
            pltpu.VMEM((8, N_TABLE), jnp.int32),
            pltpu.VMEM((1, TOK), jnp.int32),
            pltpu.SMEM((1, SEQS), jnp.int32),
            pltpu.VMEM((OWN_ITEMS, D), BF16),
            pltpu.VMEM((D, 4 * D), BF16),
            pltpu.VMEM((D, D), BF16),
            pltpu.VMEM((N_TABLE, 1, LANES), jnp.int32),
            pltpu.VMEM((N_TABLE, 1, LANES), jnp.int32),
            pltpu.VMEM(((CAP + 1) * N_TABLE, OWN_ITEMS), BF16),
            pltpu.VMEM((OWN_ITEMS, (CAP + 1) * N_TABLE), BF16),
            pltpu.VMEM((N_TABLE * CAP * CHUNKS, LANES), F32),
            pltpu.VMEM((N_TABLE, CHUNKS, LANES), F32),
            pltpu.VMEM((N_TABLE, CAP * CHUNKS, LANES), BF16),
            pltpu.VMEM((N_TABLE, CAP * CHUNKS, LANES), BF16),
            pltpu.VMEM((N_TABLE, CHUNKS, LANES), BF16),
            pltpu.VMEM((N_TABLE, CHUNKS, LANES), BF16),
            pltpu.VMEM((N_DP, N_TABLE, D), BF16),
            pltpu.VMEM((N_TABLE, D), F32),
            pltpu.VMEM((N_DP, N_TABLE, D), BF16),
            pltpu.VMEM((N_DP, N_TABLE, D), BF16),
            pltpu.VMEM((N_TABLE, CAP * CHUNKS, LANES), BF16),
            pltpu.VMEM((N_TABLE, CAP * CHUNKS, LANES), BF16),
            pltpu.VMEM((N_TABLE, CHUNKS, LANES), BF16),
            pltpu.VMEM((N_TABLE, CHUNKS, LANES), BF16),
            pltpu.VMEM((N_DP, OWN_ITEMS // 2, LANES), BF16),
            pltpu.VMEM((N_DP, OWN_ITEMS // 2, LANES), BF16),
            pltpu.SemaphoreType.DMA((7,)),
            pltpu.SemaphoreType.DMA((8,)),
            pltpu.SemaphoreType.DMA((8,)),
        ],
        compiler_params=pltpu.CompilerParams(
            collective_id=0, has_side_effects=True, vmem_limit_bytes=60 * 2**20
        ),
    )(
        jnp.transpose(request_rows[0]),
        jnp.transpose(negative_rows[0]),
        token_slots,
        item_table,
        input_weight,
        output_weight,
        history_lengths,
    )
    return loss.reshape(TOK), jnp.transpose(grad)


def solution(mesh):
    placed = (
        P("table", None),
        P(),
        P(),
        P(("dp", "table"), None, None),
        P(("dp", "table"), None, None),
        P(("dp", "table"), None),
        P(("dp", "table"), None),
    )
    return jax.shard_map(
        body,
        mesh=mesh,
        in_specs=placed,
        out_specs=(P(("dp", "table")), P("table", "dp")),
        check_vma=False,
    )
```

```python
import jax
import jax.numpy as jnp
from jax import lax
from jax.experimental import pallas as pl
from jax.experimental.pallas import tpu as pltpu
from jax.sharding import PartitionSpec as P

MESH = pl.DeviceIdType.MESH
BF16 = jnp.bfloat16
F32 = jnp.float32

N_DP = 8
N_TABLE = 64
Z_RING = 16
X_RING = 4
D = 512
HEADS = 4
HEAD = 128
TOK = 128
MAXLEN = 64
SEQS = 4
CAP = 4
OWN_ITEMS = 256
NEGS = N_DP * N_TABLE
LANES = 128
CHUNKS = D // LANES
TEMPER = 0.05


OFFSETS = sorted(
    ((x, z) for x in range(X_RING) for z in range(Z_RING)),
    key=lambda o: -(min(o[0], X_RING - o[0]) + min(o[1], Z_RING - o[1])),
)
BACK = [OFFSETS.index(((-x) % X_RING, (-z) % Z_RING)) for x, z in OFFSETS]
SELF = N_TABLE - 1
DP_ORDER = (4, 5, 2, 3, 6, 7, 1)
BACK_FAR = 24
FRONT_NEGS = 63
FRONT_ROWS = 0


def dot(a, b, contract=((1,), (0,))):
    return lax.dot_general(a, b, (contract, ((), ())), preferred_element_type=F32)


def rows_to_slabs(value, slab, slots):
    size = slots * CHUNKS
    for s in range(slots):
        for c in range(CHUNKS):
            slab[pl.ds(s * CHUNKS + c, N_TABLE, stride=size), :] = value[
                s * N_TABLE : (s + 1) * N_TABLE, c * LANES : (c + 1) * LANES
            ]


def slabs_to_rows(slab, slots):
    size = slots * CHUNKS
    rows = []
    for s in range(slots):
        parts = [
            slab[pl.ds(s * CHUNKS + c, N_TABLE, stride=size), :] for c in range(CHUNKS)
        ]
        rows.append(jnp.concatenate(parts, axis=1))
    return rows


def center_parts(values):
    middle = jnp.mean(values, axis=-1, keepdims=True)
    spread = values - middle
    scale = lax.rsqrt(jnp.mean(spread * spread, axis=-1, keepdims=True) + 1e-05)
    return spread * scale, scale


def center_back(grad, normed, scale):
    first = jnp.mean(grad, axis=-1, keepdims=True)
    second = jnp.mean(grad * normed, axis=-1, keepdims=True)
    return scale * (grad - first - normed * second)


def unit_scale(values):
    return lax.rsqrt(jnp.sum(values * values, axis=-1, keepdims=True) + 1e-06)


def unit_back(grad, values, scale):
    along = jnp.sum(grad * values, axis=-1, keepdims=True)
    return scale * grad - values * (scale * scale * scale * along)


def kernel(
    request_hbm,
    negative_hbm,
    token_hbm,
    table_hbm,
    in_weight_hbm,
    out_weight_hbm,
    length_hbm,
    loss_ref,
    grad_ref,
    request_v,
    token_v,
    length_ref,
    table_v,
    in_weight,
    out_weight,
    ask_src,
    ask_dst,
    picks,
    picks_t,
    slab_rows,
    slab_negs,
    row_src,
    row_dst,
    neg_src,
    neg_dst,
    unit_all,
    neg_raw,
    neg_out,
    neg_in,
    back_src,
    back_dst,
    neg_back_src,
    neg_back_dst,
    shard_src,
    shard_dst,
    local_sem,
    send_sem,
    recv_sem,
):
    i = lax.axis_index("dp")
    t = lax.axis_index("table")
    tx, tz = t // Z_RING, lax.rem(t, Z_RING)

    def table_peer(offset):
        return lax.rem(tx + offset[0], X_RING) * Z_RING + lax.rem(tz + offset[1], Z_RING)

    loads = [
        pltpu.make_async_copy(src, dst, local_sem.at[n])
        for n, (src, dst) in enumerate(
            (
                (request_hbm, request_v.at[pl.ds(0, CAP)]),
                (negative_hbm, request_v.at[pl.ds(CAP, 1)]),
                (token_hbm, token_v),
                (table_hbm, table_v),
                (in_weight_hbm, in_weight),
                (out_weight_hbm, out_weight),
                (length_hbm, length_ref),
            )
        )
    ]
    for load in loads:
        load.start()

    barrier = pltpu.get_barrier_semaphore()

    for offset in OFFSETS[:SELF]:
        pl.semaphore_signal(
            barrier, inc=1, device_id={"table": table_peer(offset)}, device_id_type=MESH
        )
    for k in DP_ORDER:
        pl.semaphore_signal(barrier, inc=1, device_id={"dp": i ^ k}, device_id_type=MESH)

    def send_table(src_of, dst_of, n, first=0, count=SELF):
        for k in range(first, min(first + count, SELF)):
            peer = table_peer(OFFSETS[k])
            pltpu.make_async_remote_copy(
                src_ref=src_of(k, peer),
                dst_ref=dst_of(k),
                send_sem=send_sem.at[n],
                recv_sem=recv_sem.at[n],
                device_id={"table": peer},
                device_id_type=MESH,
            ).start()

    def send_dp(src_of, dst, n):
        for k in DP_ORDER:
            peer = i ^ k
            pltpu.make_async_remote_copy(
                src_ref=src_of(peer),
                dst_ref=dst,
                send_sem=send_sem.at[n],
                recv_sem=recv_sem.at[n],
                device_id={"dp": peer},
                device_id_type=MESH,
            ).start()

    def wait_all(ref, count, n):
        part = ref.at[pl.ds(0, count)]
        pltpu.make_async_copy(part, part, recv_sem.at[n]).wait()

    def wait_sent(ref, count, n):
        part = ref.at[pl.ds(0, count)]
        pltpu.make_async_copy(part, part, send_sem.at[n]).wait()

    loads[0].wait()
    loads[1].wait()
    asks = jnp.concatenate(
        [request_v[0 : CAP + 1, :], jnp.zeros((LANES - CAP - 1, N_TABLE), jnp.int32)], axis=0
    )
    ask_src[:, 0, :] = jnp.transpose(asks.astype(F32)).astype(jnp.int32)
    ask_dst[pl.ds(SELF, 1)] = ask_src[pl.ds(t, 1)]
    pl.semaphore_wait(barrier, N_TABLE - 1 + N_DP - 1)
    send_table(lambda k, peer: ask_src.at[peer], lambda k: ask_dst.at[BACK[k]], 0)

    sub_tok = lax.broadcasted_iota(jnp.int32, (TOK, TOK), 0)
    lane_tok = lax.broadcasted_iota(jnp.int32, (TOK, TOK), 1)
    loads[6].wait()
    seg_q = jnp.zeros((TOK, TOK), jnp.int32)
    seg_k = jnp.zeros((TOK, TOK), jnp.int32)
    seg_next = jnp.zeros((TOK, TOK), jnp.int32)
    end = jnp.int32(0)
    for n in range(length_ref.shape[1]):
        end = end + length_ref[0, n]
        seg_q = seg_q + (sub_tok >= end).astype(jnp.int32)
        seg_k = seg_k + (lane_tok >= end).astype(jnp.int32)
        seg_next = seg_next + (sub_tok + 1 >= end).astype(jnp.int32)
    allowed = (seg_q == seg_k) & (lane_tok <= sub_tok)
    valid = ((seg_q == seg_next) & (sub_tok < TOK - 1))[:, 0:1]
    loads[2].wait()
    slots = token_v[...]
    place = (slots & (CAP - 1)) * N_TABLE + slots // CAP
    token_t = (
        lax.broadcasted_iota(jnp.int32, (CAP * N_TABLE, TOK), 0) == place
    ).astype(F32)
    token_pick = jnp.transpose(token_t).astype(BF16)
    token_t = token_t.astype(BF16)

    loads[3].wait()
    wait_all(ask_dst, SELF, 0)
    asked = ask_dst[:, 0, :]
    item = lax.broadcasted_iota(jnp.int32, (N_TABLE, OWN_ITEMS), 1)
    for s in range(CAP + 1):
        picks[s * N_TABLE : (s + 1) * N_TABLE, :] = (
            (asked[:, s : s + 1] == item).astype(F32)
        ).astype(BF16)
    found = dot(picks[...], table_v[...])
    for c in range(CHUNKS):
        slab_negs[:, c, :] = found[CAP * N_TABLE :, c * LANES : (c + 1) * LANES]
    neg_src[...] = slab_negs[...].astype(BF16)
    negs_out = lambda k, peer: neg_src.at[k]
    negs_at = lambda k: neg_dst.at[t]
    send_table(negs_out, negs_at, 1, 0, FRONT_NEGS)
    rows_to_slabs(found, slab_rows, CAP)
    row_src[...] = slab_rows[...].astype(BF16).reshape(row_src.shape)
    rows_out = lambda k, peer: row_src.at[k]
    rows_at = lambda k: row_dst.at[t]
    send_table(rows_out, rows_at, 2, 0, FRONT_ROWS)
    send_table(negs_out, negs_at, 1, FRONT_NEGS)
    send_table(rows_out, rows_at, 2, FRONT_ROWS)
    neg_dst[pl.ds(t, 1)] = neg_src[pl.ds(SELF, 1)]
    row_dst[pl.ds(t, 1)] = row_src[pl.ds(SELF, 1)]
    picks_t[...] = jnp.transpose(picks[...].astype(F32)).astype(BF16)

    wait_all(neg_dst, N_TABLE - 1, 1)
    slab_negs[...] = neg_dst[...].astype(F32)
    negs = jnp.concatenate([slab_negs[:, c, :] for c in range(CHUNKS)], axis=1)
    neg_raw[...] = negs
    unit_all[pl.ds(i, 1)] = (negs * unit_scale(negs)).astype(BF16)[None]
    send_dp(lambda peer: unit_all.at[i], unit_all.at[i], 3)
    loads[4].wait()
    loads[5].wait()

    wait_all(row_dst, N_TABLE - 1, 2)
    slab_rows[...] = row_dst[...].reshape(slab_rows.shape).astype(F32)
    history = jnp.concatenate(slabs_to_rows(slab_rows, CAP), axis=0).astype(BF16)
    inputs = dot(token_pick, history)
    normed, in_scale = center_parts(inputs)
    pre = dot(normed.astype(BF16), in_weight[...])
    sig = jax.nn.sigmoid(pre)
    mixed = (pre * sig).astype(BF16)
    gate, values, queries, keys = (mixed[:, n * D : (n + 1) * D] for n in range(4))
    raw, weights, attended = [], [], []
    for h in range(HEADS):
        at = slice(h * HEAD, (h + 1) * HEAD)
        scores = dot(queries[:, at], keys[:, at], ((1,), (1,))) * HEAD ** (-0.5)
        raw.append(scores)
        weight = jnp.where(allowed, scores * jax.nn.sigmoid(scores), 0.0) / MAXLEN
        weights.append(weight.astype(BF16))
        attended.append(dot(weights[h], values[:, at]))
    att_normed, att_scale = center_parts(jnp.concatenate(attended, axis=1))
    gate32 = gate.astype(F32)
    gated = (att_normed * gate32).astype(BF16)
    outputs = dot(gated, out_weight[...]) + inputs
    out_scale = unit_scale(outputs)
    unit_out = (outputs * out_scale).astype(BF16)
    item_scale = unit_scale(inputs)
    unit_items = (inputs * item_scale).astype(BF16).astype(F32)
    target = pltpu.roll(unit_items, TOK - 1, 0)
    unit_out32 = unit_out.astype(F32)
    positive = jnp.sum(unit_out32 * target, axis=1, keepdims=True) / TEMPER

    wait_all(unit_all, N_DP - 1, 3)
    unit_negs = unit_all[...].reshape(NEGS, D)
    exp_neg = jnp.exp(dot(unit_out, unit_negs, ((1,), (1,))) / TEMPER)
    exp_pos = jnp.exp(positive)
    total = exp_pos + jnp.sum(exp_neg, axis=1, keepdims=True)
    loss = jnp.where(valid, jnp.log(total) - positive, 0.0)
    loss_ref[...] = jnp.transpose(jnp.broadcast_to(loss, (TOK, LANES)))[0:1, :]

    per_row = jnp.where(valid, 1.0 / (total * TEMPER), 0.0)
    d_neg = (exp_neg * per_row).astype(BF16)
    d_pos = jnp.where(valid, exp_pos * per_row - 1.0 / TEMPER, 0.0)
    neg_out[...] = dot(d_neg, unit_out, ((0,), (0,))).astype(BF16).reshape(neg_out.shape)
    send_dp(lambda peer: neg_out.at[peer], neg_in.at[i], 4)
    neg_in[pl.ds(i, 1)] = neg_out[pl.ds(i, 1)]

    d_unit_out = dot(d_neg, unit_negs) + d_pos * target
    d_outputs = unit_back(d_unit_out, outputs, out_scale)
    d_unit_items = pltpu.roll(d_pos * unit_out32, 1, 0)
    d_inputs = d_outputs + unit_back(d_unit_items, inputs, item_scale)

    d_gated = dot(d_outputs.astype(BF16), out_weight[...], ((1,), (1,)))
    d_gate = d_gated * att_normed
    d_att = center_back(d_gated * gate32, att_normed, att_scale).astype(BF16)
    d_values, d_queries, d_keys = [], [], []
    for h in range(HEADS):
        at = slice(h * HEAD, (h + 1) * HEAD)
        d_weight = dot(d_att[:, at], values[:, at], ((1,), (1,)))
        d_values.append(dot(weights[h], d_att[:, at], ((0,), (0,))))
        s_sig = jax.nn.sigmoid(raw[h])
        slope = s_sig * (1.0 + raw[h] * (1.0 - s_sig))
        d_scores = jnp.where(
            allowed, d_weight * slope * (HEAD ** (-0.5) / MAXLEN), 0.0
        ).astype(BF16)
        d_queries.append(dot(d_scores, keys[:, at]))
        d_keys.append(dot(d_scores, queries[:, at], ((0,), (0,))))
    d_mixed = jnp.concatenate([d_gate] + d_values + d_queries + d_keys, axis=1)
    d_pre = (d_mixed * (sig * (1.0 + pre * (1.0 - sig)))).astype(BF16)
    d_normed = dot(d_pre, in_weight[...], ((1,), (1,)))
    d_inputs = d_inputs + center_back(d_normed, normed, in_scale)

    rows_to_slabs(dot(token_t, d_inputs.astype(BF16)), slab_rows, CAP)
    back_src[...] = slab_rows[...].astype(BF16).reshape(back_src.shape)
    back_dst[pl.ds(SELF, 1)] = back_src[pl.ds(t, 1)]
    rows_back = lambda k, peer: back_src.at[peer]
    rows_to = lambda k: back_dst.at[BACK[k]]
    send_table(rows_back, rows_to, 6, 0, BACK_FAR)

    wait_all(neg_in, N_DP - 1, 4)
    d_units = jnp.sum(neg_in[...].astype(F32), axis=0)
    own_negs = neg_raw[...]
    d_negs = unit_back(d_units, own_negs, unit_scale(own_negs))
    for c in range(CHUNKS):
        slab_negs[:, c, :] = d_negs[:, c * LANES : (c + 1) * LANES]
    neg_back_src[...] = slab_negs[...].astype(BF16)
    neg_back_dst[pl.ds(SELF, 1)] = neg_back_src[pl.ds(t, 1)]
    negs_back = lambda k, peer: neg_back_src.at[peer]
    negs_to = lambda k: neg_back_dst.at[BACK[k]]
    send_table(negs_back, negs_to, 5)
    send_table(rows_back, rows_to, 6, BACK_FAR)

    wait_all(neg_back_dst, N_TABLE - 1, 5)
    slab_negs[...] = neg_back_dst[...].astype(F32)
    back_negs = jnp.concatenate([slab_negs[:, c, :] for c in range(CHUNKS)], axis=1)
    wait_all(back_dst, N_TABLE - 1, 6)
    slab_rows[...] = back_dst[...].reshape(slab_rows.shape).astype(F32)
    back = slabs_to_rows(slab_rows, CAP) + [back_negs]
    shard = dot(picks_t[...], jnp.concatenate(back, axis=0).astype(BF16))

    half = OWN_ITEMS // 2
    left = lax.broadcasted_iota(jnp.int32, (half, LANES), 1) < LANES // 2
    for c in range(CHUNKS):
        top = shard[:half, c * LANES : (c + 1) * LANES]
        low = shard[half:, c * LANES : (c + 1) * LANES]
        top_r, low_r = pltpu.roll(top, LANES // 2, 1), pltpu.roll(low, LANES // 2, 1)
        shard_src[2 * c] = jnp.where(left, top, low_r).astype(BF16)
        shard_src[2 * c + 1] = jnp.where(left, top_r, low).astype(BF16)
    send_dp(lambda peer: shard_src.at[peer], shard_dst.at[i], 7)
    shard_dst[pl.ds(i, 1)] = shard_src[pl.ds(i, 1)]

    wait_sent(ask_src, N_TABLE - 1, 0)
    wait_sent(neg_src, N_TABLE - 1, 1)
    wait_sent(row_src, N_TABLE - 1, 2)
    wait_sent(unit_all, N_DP - 1, 3)
    wait_sent(neg_out, N_DP - 1, 4)
    wait_sent(neg_back_src, N_TABLE - 1, 5)
    wait_sent(back_src, N_TABLE - 1, 6)
    wait_sent(shard_src, N_DP - 1, 7)
    wait_all(shard_dst, N_DP - 1, 7)
    summed = jnp.sum(shard_dst[...].astype(F32), axis=0)
    turned = jnp.transpose(summed)
    grad_ref[:, :half] = turned[: LANES // 2, :]
    grad_ref[:, half:] = turned[LANES // 2 :, :]


def body(
    item_table,
    input_weight,
    output_weight,
    request_rows,
    negative_rows,
    token_slots,
    history_lengths,
):
    vmem = pl.BlockSpec(memory_space=pltpu.VMEM)
    anywhere = pl.BlockSpec(memory_space=pl.ANY)
    loss, grad = pl.pallas_call(
        kernel,
        name="hstu_step",
        out_shape=(
            jax.ShapeDtypeStruct((1, TOK), F32),
            jax.ShapeDtypeStruct((D // N_DP, OWN_ITEMS), F32),
        ),
        in_specs=[anywhere] * 7,
        out_specs=(vmem, vmem),
        scratch_shapes=[
            pltpu.VMEM((8, N_TABLE), jnp.int32),
            pltpu.VMEM((1, TOK), jnp.int32),
            pltpu.SMEM((1, SEQS), jnp.int32),
            pltpu.VMEM((OWN_ITEMS, D), BF16),
            pltpu.VMEM((D, 4 * D), BF16),
            pltpu.VMEM((D, D), BF16),
            pltpu.VMEM((N_TABLE, 1, LANES), jnp.int32),
            pltpu.VMEM((N_TABLE, 1, LANES), jnp.int32),
            pltpu.VMEM(((CAP + 1) * N_TABLE, OWN_ITEMS), BF16),
            pltpu.VMEM((OWN_ITEMS, (CAP + 1) * N_TABLE), BF16),
            pltpu.VMEM((N_TABLE * CAP * CHUNKS, LANES), F32),
            pltpu.VMEM((N_TABLE, CHUNKS, LANES), F32),
            pltpu.VMEM((N_TABLE, CAP * CHUNKS, LANES), BF16),
            pltpu.VMEM((N_TABLE, CAP * CHUNKS, LANES), BF16),
            pltpu.VMEM((N_TABLE, CHUNKS, LANES), BF16),
            pltpu.VMEM((N_TABLE, CHUNKS, LANES), BF16),
            pltpu.VMEM((N_DP, N_TABLE, D), BF16),
            pltpu.VMEM((N_TABLE, D), F32),
            pltpu.VMEM((N_DP, N_TABLE, D), BF16),
            pltpu.VMEM((N_DP, N_TABLE, D), BF16),
            pltpu.VMEM((N_TABLE, CAP * CHUNKS, LANES), BF16),
            pltpu.VMEM((N_TABLE, CAP * CHUNKS, LANES), BF16),
            pltpu.VMEM((N_TABLE, CHUNKS, LANES), BF16),
            pltpu.VMEM((N_TABLE, CHUNKS, LANES), BF16),
            pltpu.VMEM((N_DP, OWN_ITEMS // 2, LANES), BF16),
            pltpu.VMEM((N_DP, OWN_ITEMS // 2, LANES), BF16),
            pltpu.SemaphoreType.DMA((7,)),
            pltpu.SemaphoreType.DMA((8,)),
            pltpu.SemaphoreType.DMA((8,)),
        ],
        compiler_params=pltpu.CompilerParams(
            collective_id=0, has_side_effects=True, vmem_limit_bytes=60 * 2**20
        ),
    )(
        jnp.transpose(request_rows[0]),
        jnp.transpose(negative_rows[0]),
        token_slots,
        item_table,
        input_weight,
        output_weight,
        history_lengths,
    )
    return loss.reshape(TOK), jnp.transpose(grad)


def solution(mesh):
    placed = (
        P("table", None),
        P(),
        P(),
        P(("dp", "table"), None, None),
        P(("dp", "table"), None, None),
        P(("dp", "table"), None),
        P(("dp", "table"), None),
    )
    return jax.shard_map(
        body,
        mesh=mesh,
        in_specs=placed,
        out_specs=(P(("dp", "table")), P("table", "dp")),
        check_vma=False,
    )
```

```python
import jax
import jax.numpy as jnp
from jax import lax
from jax.experimental import pallas as pl
from jax.experimental.pallas import tpu as pltpu
from jax.sharding import PartitionSpec as P

MESH = pl.DeviceIdType.MESH
BF16 = jnp.bfloat16
F32 = jnp.float32

N_DP = 8
N_TABLE = 64
Z_RING = 16
X_RING = 4
D = 512
HEADS = 4
HEAD = 128
TOK = 128
MAXLEN = 64
SEQS = 4
CAP = 4
OWN_ITEMS = 256
NEGS = N_DP * N_TABLE
LANES = 128
CHUNKS = D // LANES
TEMPER = 0.05


OFFSETS = sorted(
    ((x, z) for x in range(X_RING) for z in range(Z_RING)),
    key=lambda o: -(min(o[0], X_RING - o[0]) + min(o[1], Z_RING - o[1])),
)
BACK = [OFFSETS.index(((-x) % X_RING, (-z) % Z_RING)) for x, z in OFFSETS]
SELF = N_TABLE - 1
DP_ORDER = (4, 5, 2, 3, 6, 7, 1)
BACK_FAR = 24
FRONT_NEGS = 63
FRONT_ROWS = 0


def dot(a, b, contract=((1,), (0,))):
    return lax.dot_general(a, b, (contract, ((), ())), preferred_element_type=F32)


def rows_to_slabs(value, slab, slots):
    size = slots * CHUNKS
    for s in range(slots):
        for c in range(CHUNKS):
            slab[pl.ds(s * CHUNKS + c, N_TABLE, stride=size), :] = value[
                s * N_TABLE : (s + 1) * N_TABLE, c * LANES : (c + 1) * LANES
            ]


def slabs_to_rows(slab, slots):
    size = slots * CHUNKS
    rows = []
    for s in range(slots):
        parts = [
            slab[pl.ds(s * CHUNKS + c, N_TABLE, stride=size), :] for c in range(CHUNKS)
        ]
        rows.append(jnp.concatenate(parts, axis=1))
    return rows


def center_parts(values):
    middle = jnp.mean(values, axis=-1, keepdims=True)
    spread = values - middle
    scale = lax.rsqrt(jnp.mean(spread * spread, axis=-1, keepdims=True) + 1e-05)
    return spread * scale, scale


def center_back(grad, normed, scale):
    first = jnp.mean(grad, axis=-1, keepdims=True)
    second = jnp.mean(grad * normed, axis=-1, keepdims=True)
    return scale * (grad - first - normed * second)


def unit_scale(values):
    return lax.rsqrt(jnp.sum(values * values, axis=-1, keepdims=True) + 1e-06)


def unit_back(grad, values, scale):
    along = jnp.sum(grad * values, axis=-1, keepdims=True)
    return scale * grad - values * (scale * scale * scale * along)


def kernel(
    small_hbm,
    table_hbm,
    in_weight_hbm,
    out_weight_hbm,
    loss_ref,
    grad_ref,
    small,
    table_v,
    in_weight,
    out_weight,
    ask_src,
    ask_dst,
    picks,
    picks_t,
    slab_rows,
    slab_negs,
    row_src,
    row_dst,
    neg_src,
    neg_dst,
    unit_all,
    neg_raw,
    neg_out,
    neg_in,
    back_src,
    back_dst,
    neg_back_src,
    neg_back_dst,
    shard_src,
    shard_dst,
    local_sem,
    send_sem,
    recv_sem,
):
    i = lax.axis_index("dp")
    t = lax.axis_index("table")
    tx, tz = t // Z_RING, lax.rem(t, Z_RING)

    def table_peer(offset):
        return lax.rem(tx + offset[0], X_RING) * Z_RING + lax.rem(tz + offset[1], Z_RING)

    loads = [
        pltpu.make_async_copy(src, dst, local_sem.at[n])
        for n, (src, dst) in enumerate(
            (
                (small_hbm, small),
                (table_hbm, table_v),
                (in_weight_hbm, in_weight),
                (out_weight_hbm, out_weight),
            )
        )
    ]
    for load in loads:
        load.start()

    barrier = pltpu.get_barrier_semaphore()

    for offset in OFFSETS[:SELF]:
        pl.semaphore_signal(
            barrier, inc=1, device_id={"table": table_peer(offset)}, device_id_type=MESH
        )
    for k in DP_ORDER:
        pl.semaphore_signal(barrier, inc=1, device_id={"dp": i ^ k}, device_id_type=MESH)

    def send_table(src_of, dst_of, n, first=0, count=SELF):
        for k in range(first, min(first + count, SELF)):
            peer = table_peer(OFFSETS[k])
            pltpu.make_async_remote_copy(
                src_ref=src_of(k, peer),
                dst_ref=dst_of(k),
                send_sem=send_sem.at[n],
                recv_sem=recv_sem.at[n],
                device_id={"table": peer},
                device_id_type=MESH,
            ).start()

    def send_dp(src_of, dst, n):
        for k in DP_ORDER:
            peer = i ^ k
            pltpu.make_async_remote_copy(
                src_ref=src_of(peer),
                dst_ref=dst,
                send_sem=send_sem.at[n],
                recv_sem=recv_sem.at[n],
                device_id={"dp": peer},
                device_id_type=MESH,
            ).start()

    def wait_all(ref, count, n):
        part = ref.at[pl.ds(0, count)]
        pltpu.make_async_copy(part, part, recv_sem.at[n]).wait()

    def wait_sent(ref, count, n):
        part = ref.at[pl.ds(0, count)]
        pltpu.make_async_copy(part, part, send_sem.at[n]).wait()

    loads[0].wait()
    asks = jnp.concatenate([small[...], jnp.zeros((LANES - 8, LANES), jnp.int32)], axis=0)
    ask_src[:, 0, :] = jnp.transpose(asks.astype(F32))[:N_TABLE, :].astype(jnp.int32)
    ask_dst[pl.ds(SELF, 1)] = ask_src[pl.ds(t, 1)]
    pl.semaphore_wait(barrier, N_TABLE - 1 + N_DP - 1)
    send_table(lambda k, peer: ask_src.at[peer], lambda k: ask_dst.at[BACK[k]], 0)

    sub_tok = lax.broadcasted_iota(jnp.int32, (TOK, TOK), 0)
    lane_tok = lax.broadcasted_iota(jnp.int32, (TOK, TOK), 1)
    seg_q = jnp.zeros((TOK, TOK), jnp.int32)
    seg_k = jnp.zeros((TOK, TOK), jnp.int32)
    seg_next = jnp.zeros((TOK, TOK), jnp.int32)
    end = jnp.zeros((1, 1), jnp.int32)
    for n in range(SEQS):
        end = end + small[CAP + 2 : CAP + 3, n : n + 1]
        seg_q = seg_q + (sub_tok >= end).astype(jnp.int32)
        seg_k = seg_k + (lane_tok >= end).astype(jnp.int32)
        seg_next = seg_next + (sub_tok + 1 >= end).astype(jnp.int32)
    allowed = (seg_q == seg_k) & (lane_tok <= sub_tok)
    valid = ((seg_q == seg_next) & (sub_tok < TOK - 1))[:, 0:1]
    slots = small[CAP + 1 : CAP + 2, :]
    place = (slots & (CAP - 1)) * N_TABLE + slots // CAP
    token_t = (
        lax.broadcasted_iota(jnp.int32, (CAP * N_TABLE, TOK), 0) == place
    ).astype(F32)
    token_pick = jnp.transpose(token_t).astype(BF16)
    token_t = token_t.astype(BF16)

    loads[1].wait()
    wait_all(ask_dst, SELF, 0)
    asked = ask_dst[:, 0, :]
    item = lax.broadcasted_iota(jnp.int32, (N_TABLE, OWN_ITEMS), 1)
    for s in range(CAP + 1):
        picks[s * N_TABLE : (s + 1) * N_TABLE, :] = (
            (asked[:, s : s + 1] == item).astype(F32)
        ).astype(BF16)
    found = dot(picks[...], table_v[...])
    for c in range(CHUNKS):
        slab_negs[:, c, :] = found[CAP * N_TABLE :, c * LANES : (c + 1) * LANES]
    neg_src[...] = slab_negs[...].astype(BF16)
    negs_out = lambda k, peer: neg_src.at[k]
    negs_at = lambda k: neg_dst.at[t]
    send_table(negs_out, negs_at, 1, 0, FRONT_NEGS)
    rows_to_slabs(found, slab_rows, CAP)
    row_src[...] = slab_rows[...].astype(BF16).reshape(row_src.shape)
    rows_out = lambda k, peer: row_src.at[k]
    rows_at = lambda k: row_dst.at[t]
    send_table(rows_out, rows_at, 2, 0, FRONT_ROWS)
    send_table(negs_out, negs_at, 1, FRONT_NEGS)
    send_table(rows_out, rows_at, 2, FRONT_ROWS)
    neg_dst[pl.ds(t, 1)] = neg_src[pl.ds(SELF, 1)]
    row_dst[pl.ds(t, 1)] = row_src[pl.ds(SELF, 1)]
    picks_t[...] = jnp.transpose(picks[...].astype(F32)).astype(BF16)

    wait_all(neg_dst, N_TABLE - 1, 1)
    slab_negs[...] = neg_dst[...].astype(F32)
    negs = jnp.concatenate([slab_negs[:, c, :] for c in range(CHUNKS)], axis=1)
    neg_raw[...] = negs
    unit_all[pl.ds(i, 1)] = (negs * unit_scale(negs)).astype(BF16)[None]
    send_dp(lambda peer: unit_all.at[i], unit_all.at[i], 3)
    loads[2].wait()
    loads[3].wait()

    wait_all(row_dst, N_TABLE - 1, 2)
    slab_rows[...] = row_dst[...].reshape(slab_rows.shape).astype(F32)
    history = jnp.concatenate(slabs_to_rows(slab_rows, CAP), axis=0).astype(BF16)
    inputs = dot(token_pick, history)
    normed, in_scale = center_parts(inputs)
    pre = dot(normed.astype(BF16), in_weight[...])
    sig = jax.nn.sigmoid(pre)
    mixed = (pre * sig).astype(BF16)
    gate, values, queries, keys = (mixed[:, n * D : (n + 1) * D] for n in range(4))
    raw, weights, attended = [], [], []
    for h in range(HEADS):
        at = slice(h * HEAD, (h + 1) * HEAD)
        scores = dot(queries[:, at], keys[:, at], ((1,), (1,))) * HEAD ** (-0.5)
        raw.append(scores)
        weight = jnp.where(allowed, scores * jax.nn.sigmoid(scores), 0.0) / MAXLEN
        weights.append(weight.astype(BF16))
        attended.append(dot(weights[h], values[:, at]))
    att_normed, att_scale = center_parts(jnp.concatenate(attended, axis=1))
    gate32 = gate.astype(F32)
    gated = (att_normed * gate32).astype(BF16)
    outputs = dot(gated, out_weight[...]) + inputs
    out_scale = unit_scale(outputs)
    unit_out = (outputs * out_scale).astype(BF16)
    item_scale = unit_scale(inputs)
    unit_items = (inputs * item_scale).astype(BF16).astype(F32)
    target = pltpu.roll(unit_items, TOK - 1, 0)
    unit_out32 = unit_out.astype(F32)
    positive = jnp.sum(unit_out32 * target, axis=1, keepdims=True) / TEMPER

    wait_all(unit_all, N_DP - 1, 3)
    unit_negs = unit_all[...].reshape(NEGS, D)
    exp_neg = jnp.exp(dot(unit_out, unit_negs, ((1,), (1,))) / TEMPER)
    exp_pos = jnp.exp(positive)
    total = exp_pos + jnp.sum(exp_neg, axis=1, keepdims=True)
    loss = jnp.where(valid, jnp.log(total) - positive, 0.0)
    loss_ref[...] = jnp.transpose(jnp.broadcast_to(loss, (TOK, LANES)))[0:1, :]

    per_row = jnp.where(valid, 1.0 / (total * TEMPER), 0.0)
    d_neg = (exp_neg * per_row).astype(BF16)
    d_pos = jnp.where(valid, exp_pos * per_row - 1.0 / TEMPER, 0.0)
    neg_out[...] = dot(d_neg, unit_out, ((0,), (0,))).astype(BF16).reshape(neg_out.shape)
    send_dp(lambda peer: neg_out.at[peer], neg_in.at[i], 4)
    neg_in[pl.ds(i, 1)] = neg_out[pl.ds(i, 1)]

    d_unit_out = dot(d_neg, unit_negs) + d_pos * target
    d_outputs = unit_back(d_unit_out, outputs, out_scale)
    d_unit_items = pltpu.roll(d_pos * unit_out32, 1, 0)
    d_inputs = d_outputs + unit_back(d_unit_items, inputs, item_scale)

    d_gated = dot(d_outputs.astype(BF16), out_weight[...], ((1,), (1,)))
    d_gate = d_gated * att_normed
    d_att = center_back(d_gated * gate32, att_normed, att_scale).astype(BF16)
    d_values, d_queries, d_keys = [], [], []
    for h in range(HEADS):
        at = slice(h * HEAD, (h + 1) * HEAD)
        d_weight = dot(d_att[:, at], values[:, at], ((1,), (1,)))
        d_values.append(dot(weights[h], d_att[:, at], ((0,), (0,))))
        s_sig = jax.nn.sigmoid(raw[h])
        slope = s_sig * (1.0 + raw[h] * (1.0 - s_sig))
        d_scores = jnp.where(
            allowed, d_weight * slope * (HEAD ** (-0.5) / MAXLEN), 0.0
        ).astype(BF16)
        d_queries.append(dot(d_scores, keys[:, at]))
        d_keys.append(dot(d_scores, queries[:, at], ((0,), (0,))))
    d_mixed = jnp.concatenate([d_gate] + d_values + d_queries + d_keys, axis=1)
    d_pre = (d_mixed * (sig * (1.0 + pre * (1.0 - sig)))).astype(BF16)
    d_normed = dot(d_pre, in_weight[...], ((1,), (1,)))
    d_inputs = d_inputs + center_back(d_normed, normed, in_scale)

    rows_to_slabs(dot(token_t, d_inputs.astype(BF16)), slab_rows, CAP)
    back_src[...] = slab_rows[...].astype(BF16).reshape(back_src.shape)
    back_dst[pl.ds(SELF, 1)] = back_src[pl.ds(t, 1)]
    rows_back = lambda k, peer: back_src.at[peer]
    rows_to = lambda k: back_dst.at[BACK[k]]
    send_table(rows_back, rows_to, 6, 0, BACK_FAR)

    wait_all(neg_in, N_DP - 1, 4)
    d_units = jnp.sum(neg_in[...].astype(F32), axis=0)
    own_negs = neg_raw[...]
    d_negs = unit_back(d_units, own_negs, unit_scale(own_negs))
    for c in range(CHUNKS):
        slab_negs[:, c, :] = d_negs[:, c * LANES : (c + 1) * LANES]
    neg_back_src[...] = slab_negs[...].astype(BF16)
    neg_back_dst[pl.ds(SELF, 1)] = neg_back_src[pl.ds(t, 1)]
    negs_back = lambda k, peer: neg_back_src.at[peer]
    negs_to = lambda k: neg_back_dst.at[BACK[k]]
    send_table(negs_back, negs_to, 5)
    send_table(rows_back, rows_to, 6, BACK_FAR)

    wait_all(neg_back_dst, N_TABLE - 1, 5)
    slab_negs[...] = neg_back_dst[...].astype(F32)
    back_negs = jnp.concatenate([slab_negs[:, c, :] for c in range(CHUNKS)], axis=1)
    wait_all(back_dst, N_TABLE - 1, 6)
    slab_rows[...] = back_dst[...].reshape(slab_rows.shape).astype(F32)
    back = slabs_to_rows(slab_rows, CAP) + [back_negs]
    shard = dot(picks_t[...], jnp.concatenate(back, axis=0).astype(BF16))

    half = OWN_ITEMS // 2
    left = lax.broadcasted_iota(jnp.int32, (half, LANES), 1) < LANES // 2
    for c in range(CHUNKS):
        top = shard[:half, c * LANES : (c + 1) * LANES]
        low = shard[half:, c * LANES : (c + 1) * LANES]
        top_r, low_r = pltpu.roll(top, LANES // 2, 1), pltpu.roll(low, LANES // 2, 1)
        shard_src[2 * c] = jnp.where(left, top, low_r).astype(BF16)
        shard_src[2 * c + 1] = jnp.where(left, top_r, low).astype(BF16)
    send_dp(lambda peer: shard_src.at[peer], shard_dst.at[i], 7)
    shard_dst[pl.ds(i, 1)] = shard_src[pl.ds(i, 1)]

    wait_sent(ask_src, N_TABLE - 1, 0)
    wait_sent(neg_src, N_TABLE - 1, 1)
    wait_sent(row_src, N_TABLE - 1, 2)
    wait_sent(unit_all, N_DP - 1, 3)
    wait_sent(neg_out, N_DP - 1, 4)
    wait_sent(neg_back_src, N_TABLE - 1, 5)
    wait_sent(back_src, N_TABLE - 1, 6)
    wait_sent(shard_src, N_DP - 1, 7)
    wait_all(shard_dst, N_DP - 1, 7)
    summed = jnp.sum(shard_dst[...].astype(F32), axis=0)
    turned = jnp.transpose(summed)
    grad_ref[:, :half] = turned[: LANES // 2, :]
    grad_ref[:, half:] = turned[LANES // 2 :, :]


def body(
    item_table,
    input_weight,
    output_weight,
    request_rows,
    negative_rows,
    token_slots,
    history_lengths,
):
    vmem = pl.BlockSpec(memory_space=pltpu.VMEM)
    anywhere = pl.BlockSpec(memory_space=pl.ANY)
    small = jnp.zeros((8, LANES), jnp.int32)
    first = 0
    for line in (
        jnp.transpose(request_rows[0]),
        jnp.transpose(negative_rows[0]),
        token_slots,
        history_lengths,
    ):
        rows, width = line.shape
        small = small + jnp.pad(line, ((first, 8 - first - rows), (0, LANES - width)))
        first += rows
    loss, grad = pl.pallas_call(
        kernel,
        name="hstu_step",
        out_shape=(
            jax.ShapeDtypeStruct((1, TOK), F32),
            jax.ShapeDtypeStruct((D // N_DP, OWN_ITEMS), F32),
        ),
        in_specs=[anywhere] * 4,
        out_specs=(vmem, vmem),
        scratch_shapes=[
            pltpu.VMEM((8, LANES), jnp.int32),
            pltpu.VMEM((OWN_ITEMS, D), BF16),
            pltpu.VMEM((D, 4 * D), BF16),
            pltpu.VMEM((D, D), BF16),
            pltpu.VMEM((N_TABLE, 1, LANES), jnp.int32),
            pltpu.VMEM((N_TABLE, 1, LANES), jnp.int32),
            pltpu.VMEM(((CAP + 1) * N_TABLE, OWN_ITEMS), BF16),
            pltpu.VMEM((OWN_ITEMS, (CAP + 1) * N_TABLE), BF16),
            pltpu.VMEM((N_TABLE * CAP * CHUNKS, LANES), F32),
            pltpu.VMEM((N_TABLE, CHUNKS, LANES), F32),
            pltpu.VMEM((N_TABLE, CAP * CHUNKS, LANES), BF16),
            pltpu.VMEM((N_TABLE, CAP * CHUNKS, LANES), BF16),
            pltpu.VMEM((N_TABLE, CHUNKS, LANES), BF16),
            pltpu.VMEM((N_TABLE, CHUNKS, LANES), BF16),
            pltpu.VMEM((N_DP, N_TABLE, D), BF16),
            pltpu.VMEM((N_TABLE, D), F32),
            pltpu.VMEM((N_DP, N_TABLE, D), BF16),
            pltpu.VMEM((N_DP, N_TABLE, D), BF16),
            pltpu.VMEM((N_TABLE, CAP * CHUNKS, LANES), BF16),
            pltpu.VMEM((N_TABLE, CAP * CHUNKS, LANES), BF16),
            pltpu.VMEM((N_TABLE, CHUNKS, LANES), BF16),
            pltpu.VMEM((N_TABLE, CHUNKS, LANES), BF16),
            pltpu.VMEM((N_DP, OWN_ITEMS // 2, LANES), BF16),
            pltpu.VMEM((N_DP, OWN_ITEMS // 2, LANES), BF16),
            pltpu.SemaphoreType.DMA((4,)),
            pltpu.SemaphoreType.DMA((8,)),
            pltpu.SemaphoreType.DMA((8,)),
        ],
        compiler_params=pltpu.CompilerParams(
            collective_id=0, has_side_effects=True, vmem_limit_bytes=215 * 2**18
        ),
    )(
        small,
        item_table,
        input_weight,
        output_weight,
    )
    return loss.reshape(TOK), jnp.transpose(grad)


def solution(mesh):
    placed = (
        P("table", None),
        P(),
        P(),
        P(("dp", "table"), None, None),
        P(("dp", "table"), None, None),
        P(("dp", "table"), None),
        P(("dp", "table"), None),
    )
    return jax.shard_map(
        body,
        mesh=mesh,
        in_specs=placed,
        out_specs=(P(("dp", "table")), P("table", "dp")),
        check_vma=False,
    )
```
